512 devices in a mesh: dp: 32 (over y, x_hi, core), tensor: 16 (over x_lo, z).
Axes of the slice: x: 4 (x_hi: 2, x_lo: 2; x = x_hi * 2 + x_lo), y: 8, z: 8, core: 2. Of those that a mesh axis runs over, the one named last changes fastest.
Arguments:
- attn: bfloat16 [4096, 4096], P('dp', 'tensor'), may hold values from -6 to 6
- residual: bfloat16 [4096, 4096], P('dp', 'tensor'), may hold values from -6 to 6
- o_weight: bfloat16 [4096, 4096], P('tensor'), may hold values from -0.09375 to 0.09375
- encoder: bfloat16 [4096, 1024], P(('dp', 'tensor')), may hold values from -0.09375 to 0.09375
- decoder: bfloat16 [1024, 4096], P(None, 'tensor'), may hold values from -0.1875 to 0.1875
- grad_out: bfloat16 [4096, 4096], P('dp', 'tensor'), may hold values from -6 to 6
Outputs:
- output: bfloat16 [4096, 4096], P('dp', 'tensor')
- grad_attn: bfloat16 [4096, 4096], P('dp', 'tensor')
- grad_weight: float32 [4096, 4096], P('tensor', 'dp')
The draws below stay inside these ranges and needn't reach their ends.
All inputs are finite; a program needn't handle non-finite values.
Results may differ from the reference program's by a relative error of at most 0.0095.
Values may be sent and summed in bfloat16 or wider, within the bound.
No kernel may reach another device: no remote copies, remote signals or barrier semaphores. Data moves between devices by JAX's collectives and lax.ppermute only.
A program may use at most 64 MiB of HBM per device.

```python
import jax
import jax.numpy as jnp
from jax import lax

D = 4096
HEADS = 32
HEAD = 128
CODE = 1024
TOKENS = 4096
N_TENSOR = 16


def levels(stream_key, extent, pieces, smallest, high):
    def one(axis_at, blocks):
        draws = jax.random.uniform(jax.random.fold_in(jax.random.fold_in(stream_key, 6), axis_at), (blocks,), jnp.float32, smallest / len(pieces), high / len(pieces))
        return jnp.repeat(jnp.exp(draws), extent[axis_at] // blocks).reshape((-1,) + (1,) * (len(extent) - axis_at - 1))

    gain = one(*pieces[0])
    for cut in pieces[1:]:
        gain = gain * one(*cut)
    return gain


def normal_values(own_key, dims, spread, most, split=(), kind=jnp.bfloat16):
    factor_of = levels(own_key, dims, split, -0.22, 0.18) if split else 1.0
    values = jax.random.normal(own_key, dims, jnp.float32) * spread * factor_of
    return jnp.minimum(jnp.maximum(values, -most), most).astype(kind)


def setup_inputs(seed: int = 0) -> dict:
    streams_of = jax.random.split(jax.random.key(seed), 7)
    return {
        "attn": normal_values(streams_of[0], (TOKENS, HEADS * HEAD), 1.0, 6.0, ((0, 32), (1, 16))),
        "residual": normal_values(streams_of[1], (TOKENS, D), 1.0, 6.0, ((0, 32), (1, 16))),
        "o_weight": normal_values(streams_of[2], (HEADS * HEAD, D), (HEADS * HEAD) ** -0.5, 0.09375, ((0, 16),)),
        "encoder": normal_values(streams_of[3], (D, CODE), D ** -0.5, 0.09375, ((0, 512),)),
        "decoder": normal_values(streams_of[4], (CODE, D), CODE ** -0.5, 0.1875, ((1, 16),)),
        "grad_out": normal_values(streams_of[5], (TOKENS, D), 1.0, 6.0, ((0, 32), (1, 16))),
    }


def reference(attn, residual, o_weight, encoder, decoder, grad_out):
    width = HEADS * HEAD
    cols = width // N_TENSOR
    folded = jnp.dot(o_weight, encoder, preferred_element_type=jnp.float32)
    attn_groups = attn.reshape(TOKENS, N_TENSOR, cols).transpose(1, 0, 2)
    folded_groups = folded.reshape(N_TENSOR, cols, CODE)

    def encode(pair):
        block, weight = pair
        value = jnp.dot(block.astype(jnp.float32), weight, precision=lax.Precision.HIGHEST)
        return value.astype(jnp.bfloat16)

    codes = lax.map(encode, (attn_groups, folded_groups))
    total_code = jnp.sum(codes.astype(jnp.float32), axis=0)
    mixed = jnp.dot(total_code, decoder.astype(jnp.float32), precision=lax.Precision.HIGHEST)
    output = (residual.astype(jnp.float32) + mixed).astype(jnp.bfloat16)
    back = jnp.dot(grad_out, decoder.T, preferred_element_type=jnp.float32).astype(jnp.bfloat16)
    grad_attn = jnp.dot(back.astype(jnp.float32), folded.T, precision=lax.Precision.HIGHEST).astype(jnp.bfloat16)
    gram = jnp.dot(attn.T, back, preferred_element_type=jnp.float32).astype(jnp.bfloat16)
    grad_weight = jnp.dot(gram, encoder.T, preferred_element_type=jnp.float32)
    return output, grad_attn, grad_weight
```

```python
import jax
import jax.numpy as jnp
from jax import lax
from jax.sharding import Mesh, PartitionSpec as P

SIZES = (8, 2, 2, 2, 8)
NAMES = ("y", "xh", "core", "xl", "z")
DP = ("y", "xh", "core")
CHIPS = ("y", "xh")
TENSOR = ("xl", "z")
SWAP = [(0, 1), (1, 0)]
F32, BF16 = jnp.float32, jnp.bfloat16


def dot(a, b, contract):
    return lax.dot_general(a, b, ((contract[:1], contract[1:]), ((), ())), preferred_element_type=F32)


def exchange(blocks, axes):
    return lax.all_to_all(blocks, axes, 0, 0)


def spread(block, n):
    return jnp.broadcast_to(block[None], (n,) + block.shape)


def total(blocks):
    return jnp.sum(blocks.astype(F32), axis=0).astype(BF16)


def in_order(core, mine, other, axis):
    return jnp.where(
        core == 0,
        jnp.concatenate([mine, other], axis),
        jnp.concatenate([other, mine], axis),
    )


def per_device(attn, residual, o_weight, encoder, decoder, grad_out):
    core = lax.axis_index("core")
    block = lax.axis_index(DP)
    mate = block + 1 - 2 * core
    half = 128

    def part(x, index, axis):
        return lax.dynamic_slice_in_dim(x, index * half, half, axis)

    attn_mine = part(attn, core, 1)
    attn_sent = part(attn, 1 - core, 1)
    attn_mate = lax.ppermute(attn_sent, "core", SWAP)

    back_term = dot(grad_out, decoder, (1, 1)).astype(BF16)
    got = exchange(
        jnp.concatenate([back_term.reshape(16, 8, 1024), spread(encoder, 16)], 1), TENSOR
    )
    enc = got[:, 8:].reshape(128, 1024)
    enc_mate = lax.ppermute(enc, "core", SWAP)
    back = exchange(spread(total(got[:, :8]), 16), TENSOR).reshape(128, 1024)
    back_mate = lax.ppermute(back, "core", SWAP)

    w_rows = part(o_weight, core, 0)
    fold_term = dot(part(w_rows, block, 1), enc, (1, 0)) + dot(part(w_rows, mate, 1), enc_mate, (1, 0))
    gram_term = dot(attn_mine, back, (0, 0)) + dot(attn_mate, back_mate, (0, 0))
    got = exchange(
        jnp.concatenate(
            [fold_term.astype(BF16).reshape(16, 8, 1024), gram_term.astype(BF16).reshape(16, 8, 1024)], 1
        ),
        CHIPS,
    )
    got = exchange(spread(total(got), 16), CHIPS)
    fold_mine = got[:, :8].reshape(128, 1024)
    gram_mine = got[:, 8:].reshape(128, 1024)
    fold_mate = lax.ppermute(fold_mine, "core", SWAP)
    gram_mate = lax.ppermute(gram_mine, "core", SWAP)

    code = (dot(attn_mine, fold_mine, (1, 0)) + dot(attn_sent, fold_mate, (1, 0))).astype(BF16)
    got = exchange(code.reshape(16, 8, 1024), TENSOR)
    total_code = exchange(spread(total(got), 16), TENSOR).reshape(128, 1024)
    mixed = dot(total_code, decoder, (1, 0))
    output = (residual.astype(F32) + mixed).astype(BF16)

    grad_attn = in_order(
        core, dot(back, fold_mine, (1, 1)).astype(BF16), dot(back, fold_mate, (1, 1)).astype(BF16), 1
    )
    grad_weight = in_order(core, dot(gram_mine, enc, (1, 1)), dot(gram_mate, enc, (1, 1)), 0)
    return output, grad_attn, grad_weight


def solution(mesh):
    fine = Mesh(mesh.devices.reshape(SIZES), NAMES)
    return jax.shard_map(
        per_device,
        mesh=fine,
        in_specs=(
            P(DP, TENSOR),
            P(DP, TENSOR),
            P(TENSOR, None),
            P(DP + TENSOR, None),
            P(None, TENSOR),
            P(DP, TENSOR),
        ),
        out_specs=(P(DP, TENSOR), P(DP, TENSOR), P(TENSOR, DP)),
        check_vma=False,
    )
```

```python
import jax
import jax.numpy as jnp
from jax import lax
from jax.sharding import Mesh, PartitionSpec as P

SIZES = (8, 2, 2, 2, 8)
NAMES = ("y", "xh", "core", "xl", "z")
DP = ("y", "xh", "core")
QUAD = ("xh", "core")
TENSOR = ("xl", "z")
F32, BF16 = jnp.float32, jnp.bfloat16


def dot(a, b, contract):
    return lax.dot_general(a, b, ((contract[:1], contract[1:]), ((), ())), preferred_element_type=F32)


def exchange(blocks, axes):
    return lax.all_to_all(blocks, axes, 0, 0)


def spread(block, n):
    return jnp.broadcast_to(block[None], (n,) + block.shape)


def total(blocks):
    return jnp.sum(blocks.astype(F32), axis=0).astype(BF16)


def together(*arrays):
    return lax.optimization_barrier(arrays)


def swap(x, axis):
    return lax.ppermute(x, axis, [(0, 1), (1, 0)])


def in_order(place, mine, other, axis):
    return jnp.where(
        place == 0, jnp.concatenate([mine, other], axis), jnp.concatenate([other, mine], axis)
    )


def per_device(attn, residual, o_weight, encoder, decoder, grad_out):
    xh, core = lax.axis_index("xh"), lax.axis_index("core")

    attn_all = attn.reshape(16, 1, 8, 256)
    attn_all = in_order(core, attn_all, swap(attn_all, "core"), 1)

    back_term = dot(grad_out, decoder, (1, 1)).astype(BF16)
    got, attn_all = together(exchange(back_term.reshape(16, 8, 1024), TENSOR), attn_all)
    rows = total(got)
    rows = jnp.concatenate([rows, encoder], 0).reshape(16, 4, 256).transpose(1, 0, 2)
    rows = exchange(rows, QUAD).reshape(4, 2, 8, 256).transpose(1, 0, 2, 3).reshape(64, 256)
    attn_all, rows = together(attn_all, rows)
    attn_all = in_order(xh, attn_all, swap(attn_all, "xh"), 1).reshape(512, 256)
    got = exchange(spread(rows, 16), TENSOR)
    back = got[:, :32].reshape(512, 256)
    enc = got[:, 32:].reshape(16, 4, 8, 256).transpose(1, 0, 2, 3).reshape(512, 256)

    w = lax.dynamic_slice_in_dim(o_weight, lax.axis_index("y") * 512, 512, 1)
    terms = [dot(w, enc, (1, 0)), dot(attn_all, back, (0, 0))]
    terms = jnp.concatenate([x.astype(BF16).reshape(8, 32, 256) for x in terms], 2)
    sums = total(exchange(terms, "y"))
    got = exchange(spread(sums, 8), "y").reshape(256, 512)
    fold, gram = got[:, :256], got[:, 256:]

    code = dot(attn_all, fold, (1, 0)).astype(BF16)
    code, fold, gram = together(code, fold, gram)
    code_rows = total(exchange(code.reshape(16, 32, 256), TENSOR))

    def split(x, place, axis):
        size = x.shape[axis] // 2
        return [lax.dynamic_slice_in_dim(x, p * size, size, axis) for p in (place, 1 - place)]

    grad_weight, weight_sent = split(dot(gram, enc, (1, 1)), xh, 1)
    grad_attn, attn_sent = split(dot(back, fold, (1, 1)).reshape(16, 4, 8, 256), xh, 1)
    came = swap(jnp.concatenate([weight_sent, attn_sent.reshape(256, 256)], 0).astype(BF16), "xh")
    rows = exchange(code_rows.reshape(4, 8, 256), QUAD)
    rows, came = together(rows, came)
    total_code = exchange(spread(rows.transpose(1, 0, 2).reshape(8, 1024), 16), TENSOR).reshape(128, 1024)
    mixed = dot(total_code, decoder, (1, 0))
    output = (residual.astype(F32) + mixed).astype(BF16)

    grad_weight, weight_sent = split(grad_weight + came[:256].astype(F32), core, 1)
    grad_attn, attn_sent = split(grad_attn + came[256:].astype(F32).reshape(16, 2, 8, 256), core, 1)
    attn_sent = attn_sent.reshape(128, 256)
    came = jnp.concatenate([weight_sent, attn_sent[:, :128], attn_sent[:, 128:]], 0)
    came = swap(came.astype(BF16), "core").astype(F32)
    grad_weight = grad_weight + came[:256]
    grad_attn = grad_attn.reshape(128, 256) + jnp.concatenate([came[256:384], came[384:]], 1)
    return output, grad_attn.astype(BF16), grad_weight


def solution(mesh):
    fine = Mesh(mesh.devices.reshape(SIZES), NAMES)
    return jax.shard_map(
        per_device,
        mesh=fine,
        in_specs=(
            P(DP, TENSOR),
            P(DP, TENSOR),
            P(TENSOR, None),
            P(DP + TENSOR, None),
            P(None, TENSOR),
            P(DP, TENSOR),
        ),
        out_specs=(P(DP, TENSOR), P(DP, TENSOR), P(TENSOR, DP)),
        check_vma=False,
    )
```

```python
import jax
import jax.numpy as jnp
from jax import lax
from jax.sharding import Mesh, PartitionSpec as P

SIZES = (8, 2, 2, 2, 8)
NAMES = ("y", "xh", "core", "xl", "z")
DP = ("y", "xh", "core")
CHIPS = ("y", "xh")
TENSOR = ("xl", "z")
SWAP = [(0, 1), (1, 0)]
F32, BF16 = jnp.float32, jnp.bfloat16


def dot(a, b, contract):
    return lax.dot_general(a, b, ((contract[:1], contract[1:]), ((), ())), preferred_element_type=F32)


def exchange(blocks, axes):
    return lax.all_to_all(blocks, axes, 0, 0)


def spread(block, n):
    return jnp.broadcast_to(block[None], (n,) + block.shape)


def total(blocks):
    return jnp.sum(blocks.astype(F32), axis=0).astype(BF16)


def together(*arrays):
    return lax.optimization_barrier(arrays)


def swap(x):
    return lax.ppermute(x, "core", SWAP)


def pair_rows(mine, mate):
    return jnp.concatenate([mine.astype(BF16).reshape(16, 8, -1), mate.astype(BF16).reshape(16, 8, -1)], 1)


def per_device(attn, residual, o_weight, encoder, decoder, grad_out):
    core = lax.axis_index("core")
    block = lax.axis_index(DP)
    starts = [x.astype(jnp.uint32) for x in (block * 128, (block + 1 - 2 * core) * 128, core * 512, 512 - core * 512)]

    def part(x, start, size, axis):
        return lax.dynamic_slice_in_dim(x, start, size, axis)

    back_term = dot(grad_out, decoder, (1, 1)).astype(BF16)
    enc_mine, enc_sent = part(encoder, starts[2], 512, 1), part(encoder, starts[3], 512, 1)
    got, attn_mate, enc_mine, enc_sent, core_is_0, *starts = together(
        exchange(back_term.reshape(16, 8, 1024), TENSOR), swap(attn), enc_mine, enc_sent, core == 0, *starts
    )
    rows = total(got)
    came = swap(jnp.concatenate([part(rows, starts[3], 512, 1), enc_sent], 0))
    rows = jnp.concatenate([part(rows, starts[2], 512, 1), enc_mine, came], 0)
    got = exchange(spread(rows, 16), TENSOR)
    back, enc, back_mate, enc_mate = [got[:, i : i + 8].reshape(128, 512) for i in (0, 8, 16, 24)]

    fold_term = dot(part(o_weight, starts[0], 128, 1), enc, (1, 0)) + dot(part(o_weight, starts[1], 128, 1), enc_mate, (1, 0))
    gram_term = dot(attn, back, (0, 0)) + dot(attn_mate, back_mate, (0, 0))
    got = exchange(
        jnp.concatenate([fold_term.astype(BF16), gram_term.astype(BF16)], 1).reshape(16, 16, 1024), CHIPS
    )
    got = exchange(spread(total(got), 16), CHIPS).reshape(256, 1024)
    fold, gram = got[:, :512], got[:, 512:]

    code = pair_rows(dot(attn, fold, (1, 0)), dot(attn_mate, fold, (1, 0)))
    code, fold, gram = together(code, fold, gram)
    rows = total(exchange(code, TENSOR))
    mine, came = rows[:8], swap(rows[8:])
    rows = jnp.where(core_is_0, jnp.concatenate([mine, came], 1), jnp.concatenate([came, mine], 1))
    total_code = exchange(spread(rows, 16), TENSOR).reshape(128, 1024)
    mixed = dot(total_code, decoder, (1, 0))
    output = (residual.astype(F32) + mixed).astype(BF16)

    attn_term = dot(back_mate, fold, (1, 1))
    terms = swap(jnp.concatenate([dot(gram, enc_mate, (1, 1)), attn_term[:, :128], attn_term[:, 128:]], 0))
    grad_weight = dot(gram, enc, (1, 1)) + terms[:256]
    grad_attn = dot(back, fold, (1, 1)) + jnp.concatenate([terms[256:384], terms[384:]], 1)
    return output, grad_attn.astype(BF16), grad_weight


def solution(mesh):
    fine = Mesh(mesh.devices.reshape(SIZES), NAMES)
    return jax.shard_map(
        per_device,
        mesh=fine,
        in_specs=(
            P(DP, TENSOR),
            P(DP, TENSOR),
            P(TENSOR, None),
            P(DP + TENSOR, None),
            P(None, TENSOR),
            P(DP, TENSOR),
        ),
        out_specs=(P(DP, TENSOR), P(DP, TENSOR), P(TENSOR, DP)),
        check_vma=False,
    )
```

```python
import jax
import jax.numpy as jnp
from jax import lax
from jax.sharding import Mesh, PartitionSpec as P

SIZES = (8, 2, 2, 2, 8)
NAMES = ("y", "xh", "core", "xl", "z")
DP = ("y", "xh", "core")
CHIPS = ("xh", "y")
TENSOR = ("xl", "z")
SWAP = [(0, 1), (1, 0)]
F32, BF16 = jnp.float32, jnp.bfloat16


def dot(a, b, contract):
    return lax.dot_general(a, b, ((contract[:1], contract[1:]), ((), ())), preferred_element_type=F32)


def exchange(blocks, axes):
    return lax.all_to_all(blocks, axes, 0, 0)


def spread(block, n):
    return jnp.broadcast_to(block[None], (n,) + block.shape)


def total(blocks):
    return jnp.sum(blocks.astype(F32), axis=0).astype(BF16)


def together(*arrays):
    return lax.optimization_barrier(arrays)


def swap(x):
    return lax.ppermute(x, "core", SWAP)


def pair_rows(mine, mate):
    return jnp.concatenate([mine.astype(BF16).reshape(16, 8, -1), mate.astype(BF16).reshape(16, 8, -1)], 1)


def per_device(attn, residual, o_weight, encoder, decoder, grad_out):
    core = lax.axis_index("core")
    block = lax.axis_index(DP)
    starts = [x.astype(jnp.uint32) for x in (block * 128, (block + 1 - 2 * core) * 128, core * 512, 512 - core * 512)]

    def part(x, start, size, axis):
        return lax.dynamic_slice_in_dim(x, start, size, axis)

    back_term = dot(grad_out, decoder, (1, 1)).astype(BF16)
    enc_mine, enc_sent = part(encoder, starts[2], 512, 1), part(encoder, starts[3], 512, 1)
    got, attn_mate, enc_mine, enc_sent, core_is_0, *starts = together(
        exchange(back_term.reshape(16, 8, 1024), TENSOR), swap(attn), enc_mine, enc_sent, core == 0, *starts
    )
    rows = total(got)
    came = swap(jnp.concatenate([part(rows, starts[3], 512, 1), enc_sent], 0))
    rows = jnp.concatenate([part(rows, starts[2], 512, 1), enc_mine, came], 0)
    got = exchange(spread(rows, 16), TENSOR)
    back, enc, back_mate, enc_mate = [got[:, i : i + 8].reshape(128, 512) for i in (0, 8, 16, 24)]

    fold_term = dot(part(o_weight, starts[0], 128, 1), enc, (1, 0)) + dot(part(o_weight, starts[1], 128, 1), enc_mate, (1, 0))
    gram_term = dot(attn, back, (0, 0)) + dot(attn_mate, back_mate, (0, 0))
    got = exchange(
        jnp.concatenate([fold_term.astype(BF16), gram_term.astype(BF16)], 1).reshape(16, 16, 1024), CHIPS
    )
    got = exchange(spread(total(got), 16), CHIPS).reshape(256, 1024)
    fold, gram = got[:, :512], got[:, 512:]

    code = pair_rows(dot(attn, fold, (1, 0)), dot(attn_mate, fold, (1, 0)))
    code, fold, gram = together(code, fold, gram)
    rows = total(exchange(code, TENSOR))
    mine, came = rows[:8], swap(rows[8:])
    rows = jnp.where(core_is_0, jnp.concatenate([mine, came], 1), jnp.concatenate([came, mine], 1))
    total_code = exchange(spread(rows, 16), TENSOR).reshape(128, 1024)
    mixed = dot(total_code, decoder, (1, 0))
    output = (residual.astype(F32) + mixed).astype(BF16)

    attn_term = dot(back_mate, fold, (1, 1))
    terms = swap(jnp.concatenate([dot(gram, enc_mate, (1, 1)), attn_term[:, :128], attn_term[:, 128:]], 0))
    grad_weight = dot(gram, enc, (1, 1)) + terms[:256]
    grad_attn = dot(back, fold, (1, 1)) + jnp.concatenate([terms[256:384], terms[384:]], 1)
    return output, grad_attn.astype(BF16), grad_weight


def solution(mesh):
    fine = Mesh(mesh.devices.reshape(SIZES), NAMES)
    return jax.shard_map(
        per_device,
        mesh=fine,
        in_specs=(
            P(DP, TENSOR),
            P(DP, TENSOR),
            P(TENSOR, None),
            P(DP + TENSOR, None),
            P(None, TENSOR),
            P(DP, TENSOR),
        ),
        out_specs=(P(DP, TENSOR), P(DP, TENSOR), P(TENSOR, DP)),
        check_vma=False,
    )
```
